256 devices in a mesh: rec: 32 (over x_lo, z, core), tm: 8 (over y, x_hi).
Axes of the slice: x: 4 (x_hi: 2, x_lo: 2; x = x_hi * 2 + x_lo), y: 4, z: 8, core: 2. Of those that a mesh axis runs over, the one named last changes fastest.
Arguments:
- frames_in: bfloat16 [64, 512, 1536], P('rec', 'tm'), parts along dimension 0, may hold values from -6 to 6
- lengths: int32 [64], P('rec'), parts along dimension 0, may hold values from 128 to 512, as said below
- ln1_gain: float32 [1536], replicated, may hold values from 0.5 to 1.5
- w_qkv: bfloat16 [3, 1536, 1536], P(None, 'tm'), may hold values from -0.15625 to 0.15625
- bias_u: float32 [16, 96], P('tm'), may hold values from -3 to 3
- bias_v: float32 [16, 96], P('tm'), may hold values from -8 to 8
- pos_keys: bfloat16 [1536, 1024], P('tm'), may hold values from -8 to 8
- w_out: bfloat16 [1536, 1536], P('tm'), may hold values from -0.625 to 0.625
- ln2_gain: float32 [1536], replicated, may hold values from 0.5 to 1.5
- w_glu: bfloat16 [2, 1536, 1536], P(None, 'tm'), may hold values from -0.15625 to 0.15625
- depth_kernel: float32 [31, 1536], replicated, may hold values from -1 to 1
- bn_scale: float32 [1536], replicated, may hold values from 0.25 to 1.75
- bn_shift: float32 [1536], replicated, may hold values from -3 to 3
Outputs:
- attended: bfloat16 [64, 512, 1536], P('rec', 'tm'), parts along dimension 0
- conv_out: bfloat16 [64, 512, 1536], P('rec', 'tm'), parts along dimension 0
The draws below stay inside these ranges and needn't reach their ends.
There are 32 independent parts, one for each index of `rec`. The reference program is written for one: setup_inputs(seed, part) draws one part's arguments, and reference() takes and returns one part's arrays. A program takes and returns all parts, laid end to end along the dimension named above; an argument that names none is the same for every part. Nothing has to cross between parts.
Inputs may be any that keep to these rules, and one draw needn't show every extreme that they name: `lengths`: each recording's count of valid frames from its start; in every part one recording is full (512).
All inputs are finite; a program needn't handle non-finite values.
Results may differ from the reference program's by a relative error of at most 0.012.
Values may be sent and summed in bfloat16 or wider, within the bound.
A program may use at most 128 MiB of HBM per device.

```python
import math
import jax
import jax.numpy as jnp
from jax import lax

D = 1536
H = 16
DH = 96
KERNEL = 31
REC = 2
FRAMES = 512


def draw_lengths(key, part):
    key = jax.random.fold_in(key, 5)
    keys = jax.random.split(key, 2)
    counts = jax.random.randint(keys[0], (REC,), FRAMES // 4, FRAMES + 1)
    full = jax.random.randint(keys[1], (), 0, REC)
    return jnp.where(jnp.arange(REC) == full, FRAMES, counts).astype(jnp.int32)


def draw_bias_v(key, part):
    key = jax.random.fold_in(key, 4)
    noise = jnp.clip(jax.random.normal(key, (H, DH), jnp.float32), -6.0, 6.0)
    return 0.5 * noise


def draw_pos_keys(key, part):
    key = jax.random.fold_in(key, 3)
    base = jnp.clip(jax.random.normal(key, (H * DH, 2 * FRAMES), jnp.float32), -4.5, 4.5)
    return base.astype(jnp.bfloat16)


def level_of(key, extent, cuts, low, largest):
    loudness, own = 1.0, jax.random.fold_in(key, 6)
    for axis_at, parts in cuts:
        heights = jnp.exp(jax.random.uniform(jax.random.fold_in(own, axis_at), (parts,), jnp.float32, low / len(cuts), largest / len(cuts)))
        loudness = loudness * jnp.repeat(heights, extent[axis_at] // parts).reshape([-1 if axis == axis_at else 1 for axis in range(len(extent))])
    return loudness


def normal_values(rng, dims, spread, most, shards=(), kind=jnp.bfloat16):
    array = spread * jax.random.normal(rng, dims, jnp.float32)
    if shards:
        array = array * level_of(rng, dims, shards, -0.22, 0.18)
    return jnp.clip(array, -most, most).astype(kind)


def setup_inputs(seed: int = 0, part: int = 0) -> dict:
    streams_of = jax.random.split(jax.random.key(seed), 14)
    part_keys = jax.random.split(jax.random.fold_in(streams_of[13], part), 14)
    frames_in = normal_values(part_keys[0], (REC, FRAMES, D), 1.0, 6.0, ((1, 8),))
    lengths = draw_lengths(jax.random.fold_in(jax.random.fold_in(streams_of[13], part), 71), part)
    ln1_gain = jnp.clip(1.0 + 0.1 * jax.random.normal(streams_of[2], (D,), jnp.float32), 0.5, 1.5)
    w_qkv = normal_values(streams_of[3], (3, H * DH, D), D ** -0.5, 0.15625, ((1, 8),))
    bias_u = normal_values(streams_of[4], (H, DH), 0.5, 3.0, ((0, 8),), jnp.float32)
    bias_v = draw_bias_v(jax.random.fold_in(streams_of[13], 71), part)
    pos_keys = draw_pos_keys(jax.random.fold_in(streams_of[13], 71), part)
    w_out = normal_values(streams_of[7], (H * DH, D), (H * DH // 16) ** -0.5, 0.625, ((0, 8),))
    ln2_gain = jnp.clip(1.0 + 0.1 * jax.random.normal(streams_of[8], (D,), jnp.float32), 0.5, 1.5)
    w_glu = normal_values(streams_of[9], (2, D, D), D ** -0.5, 0.15625, ((1, 8),))
    depth_kernel = normal_values(streams_of[10], (KERNEL, D), KERNEL ** -0.5, 1.0, (), jnp.float32)
    bn_scale = jnp.clip(1.0 + 0.15 * jax.random.normal(streams_of[11], (D,), jnp.float32), 0.25, 1.75)
    bn_shift = normal_values(streams_of[12], (D,), 0.5, 3.0, (), jnp.float32)
    return {"frames_in": frames_in, "lengths": lengths, "ln1_gain": ln1_gain, "w_qkv": w_qkv, "bias_u": bias_u, "bias_v": bias_v, "pos_keys": pos_keys, "w_out": w_out, "ln2_gain": ln2_gain, "w_glu": w_glu, "depth_kernel": depth_kernel, "bn_scale": bn_scale, "bn_shift": bn_shift}


def layer_norm(values, gain):
    wide = values.astype(jnp.float32)
    mean = lax.optimization_barrier(jnp.mean(wide, axis=-1, keepdims=True))
    centered = wide - mean
    variance = lax.optimization_barrier(jnp.mean(centered * centered, axis=-1, keepdims=True))
    return centered * lax.rsqrt(variance + 1e-05) * gain

def skew_rows(matrix, frames):
    block, width = (matrix.shape[-2], matrix.shape[-1])
    flat = matrix.reshape(matrix.shape[:-2] + (block * width,))
    moved = flat[..., block - 1:block - 1 + block * (width - 1)]
    return moved.reshape(matrix.shape[:-2] + (block, width - 1))[..., :frames]

def attend(qkv, bias_u, bias_v, pos_keys, length):
    heads, head_dim = bias_u.shape
    frames = qkv.shape[0]
    block = min(512, frames)
    count = frames // block
    scale = 1.0 / math.sqrt(head_dim)
    query = qkv[:, 0].reshape(frames, heads, head_dim)
    keys = qkv[:, 1].reshape(frames, heads, head_dim).astype(jnp.float32)
    values = qkv[:, 2].reshape(frames, heads, head_dim).astype(jnp.float32)
    position = pos_keys.reshape(heads, head_dim, 2 * frames)
    key_valid = jnp.arange(frames) < length

    def one_block(index):
        start = (index * block).astype(jnp.int32)
        rows = lax.dynamic_slice_in_dim(query, start, block, 0).astype(jnp.float32)
        query_u = (rows + bias_u).astype(jnp.bfloat16).astype(jnp.float32)
        query_v = (rows + bias_v).astype(jnp.bfloat16).astype(jnp.float32)
        content = jnp.einsum('bhd,jhd->hbj', query_u, keys)
        window = lax.dynamic_slice_in_dim(position, (frames - start - block).astype(jnp.int32), frames + block - 1, 2)
        relative = skew_rows(jnp.einsum('bhd,hdw->hbw', query_v, window.astype(jnp.float32)), frames)
        scores = (content + relative) * scale
        scores = jnp.where(key_valid[None, None, :], scores, -1e+30)
        peak = lax.optimization_barrier(jnp.max(scores, axis=-1, keepdims=True))
        expd = jnp.exp(scores - peak)
        total = lax.optimization_barrier(jnp.sum(expd, axis=-1, keepdims=True))
        weights = (expd / total).astype(jnp.bfloat16).astype(jnp.float32)
        mixed = jnp.einsum('hbj,jhd->bhd', weights, values)
        return mixed.astype(jnp.bfloat16).reshape(block, heads * head_dim)
    outputs = lax.map(one_block, jnp.arange(count, dtype=jnp.int32))
    return outputs.reshape(frames, heads * head_dim)

def reference(frames_in, lengths, ln1_gain, w_qkv, bias_u, bias_v, pos_keys, w_out, ln2_gain, w_glu, depth_kernel, bn_scale, bn_shift):
    normed = layer_norm(frames_in, ln1_gain).astype(jnp.bfloat16)
    qkv = jnp.einsum('rfd,kcd->rfkc', normed.astype(jnp.float32), w_qkv.astype(jnp.float32)).astype(jnp.bfloat16)
    heads_out = jnp.stack([attend(qkv[index], bias_u, bias_v, pos_keys, lengths[index]) for index in range(REC)])
    projected = jnp.einsum('rfc,cd->rfd', heads_out.astype(jnp.float32), w_out.astype(jnp.float32))
    attended = (frames_in.astype(jnp.float32) + projected).astype(jnp.bfloat16)
    normed2 = layer_norm(attended, ln2_gain).astype(jnp.bfloat16).astype(jnp.float32)
    first = jnp.einsum('rfd,cd->rfc', normed2, w_glu[0].astype(jnp.float32))
    second = jnp.einsum('rfd,cd->rfc', normed2, w_glu[1].astype(jnp.float32))
    gated = first * jax.nn.sigmoid(second)
    valid = jnp.arange(FRAMES)[None, :] < lengths[:, None]
    gated = jnp.where(valid[:, :, None], gated, 0.0).astype(jnp.bfloat16)
    half = KERNEL // 2
    padded = jnp.pad(gated, ((0, 0), (half, half), (0, 0)))
    summed = jnp.zeros(gated.shape, jnp.float32)
    for offset in range(KERNEL):
        summed = summed + padded[:, offset:offset + FRAMES].astype(jnp.float32) * depth_kernel[offset]
    shifted = summed * bn_scale + bn_shift
    conv_out = (shifted * jax.nn.sigmoid(shifted)).astype(jnp.bfloat16)
    return (attended, conv_out)
```

```python
import functools
import math

import jax
import jax.numpy as jnp
from jax import lax
from jax.experimental import pallas as pl
from jax.experimental.pallas import tpu as pltpu
from jax.sharding import PartitionSpec as P

MESH = pl.DeviceIdType.MESH
F32, BF16 = jnp.float32, jnp.bfloat16
PEERS = 8
Z_CHIPS = 8
FD = 64
FRAMES = 512
D = 1536
CH = 192
DH = 96
TAPS = 31
NT = (((1,), (1,)), ((), ()))
NN = (((1,), (0,)), ((), ()))
SCALE2 = math.log2(math.e) / math.sqrt(DH)


def dot(a, b, dims=NN):
    return lax.dot_general(a, b, dims, preferred_element_type=F32)


def norm_rows(values, gain):
    mean = jnp.mean(values, axis=-1, keepdims=True)
    centered = values - mean
    variance = jnp.mean(centered * centered, axis=-1, keepdims=True)
    return (centered * lax.rsqrt(variance + 1e-05) * gain).astype(BF16)


def sigmoid(v):
    return 1.0 / (1.0 + jnp.exp(-v))


def kernel(
    frames_hbm, lengths, gain1, w_qkv_hbm, bias_u, bias_v, pos_hbm, w_out_hbm, gain2, w_glu_hbm,
    taps_ref, scale_ref, shift_ref,
    attended, conv_out,
    x, nrm, n2, wq, wg, wo, pos, qkv, vext, hs, hb, gp, cs, cb, bias_s, taps_s, bn_s,
    local_sem, ag_send, ag_recv, aa_send, aa_recv, wo_send, wo_recv,
):
    rec, me = lax.axis_index("rec"), lax.axis_index("tm")
    y, xh = me // 2, lax.rem(me, 2)
    core, z = lax.rem(rec, 2), lax.rem(rec // 2, Z_CHIPS)
    x_lo = rec // (2 * Z_CHIPS)

    def rec_of(zz, cc):
        return (x_lo * Z_CHIPS + lax.rem(zz + Z_CHIPS, Z_CHIPS)) * 2 + cc

    def slot(dy, flip):
        return lax.rem(y + dy, 4) * 2 + (1 - xh if flip else xh)

    s_x, s_up, s_dn, s_far = slot(0, True), slot(1, False), slot(3, False), slot(2, False)
    s_upx, s_dnx, s_farx = slot(1, True), slot(3, True), slot(2, True)
    z_up, z_dn, sibling = rec_of(z + 1, core), rec_of(z - 1, core), rec_of(z, 1 - core)

    def remote(src, dst, send, recv, device):
        return pltpu.make_async_remote_copy(
            src_ref=src, dst_ref=dst, send_sem=send, recv_sem=recv, device_id=device,
            device_id_type=MESH,
        )

    quarter = lax.rem(z, 4)
    wo_rows = pl.ds(pl.multiple_of(quarter * 48, 16), 48)
    wo_cols = pl.ds(pl.multiple_of(core * 768, 128), 768)
    loads = [
        (frames_hbm.at[0], x.at[0]),
        (frames_hbm.at[1], x.at[1]),
        (w_out_hbm.at[wo_rows, wo_cols], wo.at[me, wo_rows, wo_cols]),
        (w_qkv_hbm.at[0, pl.ds(0, DH)], wq.at[pl.ds(0, DH)]),
        (w_qkv_hbm.at[0, pl.ds(DH, DH)], wq.at[pl.ds(128, DH)]),
        (w_qkv_hbm.at[1, pl.ds(0, DH)], wq.at[pl.ds(256, DH)]),
        (w_qkv_hbm.at[1, pl.ds(DH, DH)], wq.at[pl.ds(384, DH)]),
        (w_qkv_hbm.at[2], wq.at[pl.ds(512, CH)]),
        (pos_hbm.at[pl.ds(0, DH)], pos.at[0, pl.ds(0, DH)]),
        (pos_hbm.at[pl.ds(DH, DH)], pos.at[1, pl.ds(0, DH)]),
        (w_glu_hbm.at[0], wg.at[pl.ds(0, CH)]),
        (w_glu_hbm.at[1], wg.at[pl.ds(256, CH)]),
    ]
    loads = [pltpu.make_async_copy(s, d, local_sem.at[i]) for i, (s, d) in enumerate(loads)]
    for load in loads:
        load.start()

    barrier = pltpu.get_barrier_semaphore()
    for step in range(1, PEERS):
        pl.semaphore_signal(
            barrier, inc=1, device_id=(rec, lax.rem(me + step, PEERS)), device_id_type=MESH
        )
    for other in (z_up, z_dn, sibling):
        pl.semaphore_signal(barrier, inc=1, device_id=(other, me), device_id_type=MESH)

    def ag(which, buf, r, index, arriving=False):
        low, high = (pl.ds(0, 32),), (pl.ds(32, 32),)
        plan = [
            (me, (), s_x, s_x),
            (me, (), s_up, s_dn),
            (me, (), s_dn, s_up),
            (s_x, (), s_up, s_dnx),
            (s_x, (), s_dn, s_upx),
            (s_dn, low, s_up, s_far),
            (s_up, high, s_dn, s_far),
            (s_far, low, s_x, s_farx),
            (s_far, high, s_x, s_farx),
        ]
        src, rows, target, landing = plan[index]
        sems = (ag_send.at[which, r, index], ag_recv.at[which, r, index])
        part = buf.at[(r, landing if arriving else src) + rows]
        return remote(part, part, *sems, (rec, target))

    def ag_start(which, buf, r, *indices):
        for index in indices:
            ag(which, buf, r, index).start()

    def ag_wait(which, buf, r, *indices):
        for index in indices:
            ag(which, buf, r, index, True).wait_recv()

    def ag_first(which, buf, r):
        ag_start(which, buf, r, 0, 1, 2)

    def ag_second(which, buf, r):
        ag_wait(which, buf, r, 1)
        ag_start(which, buf, r, 5)
        ag_wait(which, buf, r, 2)
        ag_start(which, buf, r, 6)
        ag_wait(which, buf, r, 0)
        ag_start(which, buf, r, 3, 4)

    def ag_third(which, buf, r):
        ag_wait(which, buf, r, 5)
        ag_start(which, buf, r, 7)
        ag_wait(which, buf, r, 6)
        ag_start(which, buf, r, 8)

    def ag_finish(which, buf, r):
        ag_wait(which, buf, r, 3, 4, 7, 8)

    def aa(which, out, into, r, step, arriving=False):
        to, source = lax.rem(me + step, PEERS), lax.rem(me + PEERS - step, PEERS)
        sems = (aa_send.at[which, r, step], aa_recv.at[which, r, step])
        return remote(out.at[r, to], into.at[r, source if arriving else me], *sems, (rec, to))

    def aa_start(which, out, into, r):
        for step in range(1, PEERS):
            aa(which, out, into, r, step).start()
        into[r, me] = out[r, me]

    def aa_wait(which, out, into, r):
        for step in range(1, PEERS):
            aa(which, out, into, r, step, True).wait_recv()

    def wo_set(q, c, half=None):
        width = 768 if half is None else 384
        start = c * 768 + (0 if half is None else half * 384)
        return wo.at[
            :,
            pl.ds(pl.multiple_of(lax.rem(q + 4, 4) * 48, 16), 48),
            pl.ds(pl.multiple_of(start, 128), width),
        ]

    def wo_copy(index, arriving=False):
        sems = (wo_send.at[index], wo_recv.at[index])
        if index < 7:
            step = index + 1
            to, source = lax.rem(me + step, PEERS), lax.rem(me + PEERS - step, PEERS)
            mine = wo.at[me, wo_rows, wo_cols]
            landed = wo.at[source, wo_rows, wo_cols]
            device = (rec, to)
        elif index < 11:
            q_sent, half, q_land, to = [
                (quarter, None, quarter - 1, z_up),
                (quarter, None, quarter + 1, z_dn),
                (quarter - 1, 0, quarter - 2, z_up),
                (quarter + 1, 1, quarter + 2, z_dn),
            ][index - 7]
            mine, landed = wo_set(q_sent, core, half), wo_set(q_land, core, half)
            device = (to, me)
        else:
            q, half = [
                (quarter, None), (quarter - 1, None), (quarter + 1, None),
                (quarter - 2, 0), (quarter + 2, 1),
            ][index - 11]
            mine, landed = wo_set(q, core, half), wo_set(q, 1 - core, half)
            device = (sibling, me)
        part = landed if arriving else mine
        return remote(part, part, *sems, device)

    def wo_start(*indices):
        for index in indices:
            wo_copy(index).start()

    def wo_wait(*indices):
        for index in indices:
            wo_copy(index, True).wait_recv()

    def first_norm(r):
        nrm[r, me] = norm_rows(x[r].astype(F32), gain1[...])

    def project(r):
        rows = nrm.at[r]

        @pl.loop(0, 3)
        def _(n):
            cols = pl.ds(pl.multiple_of(n * 256, 256), 256)
            part = dot(rows[...].reshape(FRAMES, D), wq[cols, :], NT)
            qkv[:, cols] = part.astype(BF16)

        v = qkv[:, pl.ds(512, 256)].astype(F32)
        lane = lax.broadcasted_iota(jnp.int32, v.shape, 1)
        ones = jnp.where(lane == CH, 1.0, 0.0)
        vext[0] = jnp.where(lane < DH, v, ones).astype(BF16)
        vext[1] = jnp.where((lane >= DH) & (lane < CH), v, ones).astype(BF16)

    def attend(r):
        valid = lax.broadcasted_iota(jnp.int32, (128, FRAMES), 1) < lengths[r]

        @pl.loop(0, 4)
        def _(block):
            mixed = []
            for h in range(2):
                q = qkv[pl.ds(pl.multiple_of(block * 128, 128), 128), pl.ds(h * 128, 128)].astype(F32)
                query_u = (q + bias_s[0, pl.ds(h, 1), :]).astype(BF16)
                query_v = (q + bias_s[1, pl.ds(h, 1), :]).astype(BF16)
                content = dot(query_u, qkv[:, pl.ds(256 + h * 128, 128)], NT)
                window = pos[h, :, pl.ds(pl.multiple_of(384 - block * 128, 128), 640)]
                relative = dot(query_v, window)
                relative = pltpu.roll(relative, 513, 1, stride=1, stride_axis=0)[:, :FRAMES]
                scores = jnp.where(valid, content + relative, -1e30)
                peak = jnp.max(scores, axis=-1, keepdims=True)
                expd = jnp.exp2((scores - peak) * SCALE2).astype(BF16)
                out = dot(expd, vext[h])
                mixed.append(out / out[:, CH : CH + 1])
            lane = lax.broadcasted_iota(jnp.int32, mixed[0].shape, 1)
            both = jnp.where(lane < DH, mixed[0], mixed[1])[:, :CH].astype(BF16)
            hs[r, 2 * block] = both[:FD]
            hs[r, 2 * block + 1] = both[FD:]

    def out_project(r):
        heads = jnp.concatenate([hb[r, s] for s in range(PEERS)], axis=-1)
        for n in range(3):
            cols = pl.ds(n * 512, 512)
            part = dot(heads, wo[:, :, cols].reshape(D, 512))
            attended[r, :, cols] = (x[r, :, cols].astype(F32) + part).astype(BF16)
        n2[r, me] = norm_rows(attended[r].astype(F32), gain2[...])

    def glu(r):
        @pl.loop(0, 4)
        def _(block):
            rows = n2[r, pl.ds(block * 2, 2)].reshape(128, D)
            both = dot(rows, wg[...], NT)
            gated = both[:, :256] * sigmoid(both[:, 256:])
            frame = block * 128 + lax.broadcasted_iota(jnp.int32, gated.shape, 0)
            gated = jnp.where(frame < lengths[r], gated, 0.0).astype(BF16).astype(F32)
            at = pl.ds(pl.multiple_of(16 + block * 128, 16), 128)
            gp[0, at, :] = gated[:, :128]
            gp[1, at, :] = gated[:, 128:]

    def conv(r):
        @pl.loop(0, PEERS)
        def _(block):
            for c in range(2):
                total = jnp.zeros((FD, 128), F32)
                for t in range(TAPS):
                    total += gp[c, pl.ds(block * FD + t + 1, FD), :] * taps_s[c, pl.ds(t, 1), :]
                s = total * bn_s[0, pl.ds(c, 1), :] + bn_s[1, pl.ds(c, 1), :]
                out = (s * sigmoid(s)).astype(BF16)
                if c == 0:
                    cs[r, block, :, pl.ds(0, 128)] = out
                else:
                    cs[r, block, :, pl.ds(128, 64)] = out[:, :64]

    def conv_finish(r):
        conv_out[r] = jnp.concatenate([cb[r, s] for s in range(PEERS)], axis=-1)

    def prepare():
        for start in (96, 224, 352, 480):
            wq[pl.ds(start, 32), :] = jnp.zeros((32, D), BF16)
        wq[pl.ds(704, 64), :] = jnp.zeros((64, D), BF16)
        for start in (192, 448):
            wg[pl.ds(start, 64), :] = jnp.zeros((64, D), BF16)
        for h in range(2):
            pos[h, pl.ds(DH, 32), :] = jnp.zeros((32, 2 * FRAMES), BF16)
        bias_s[...] = jnp.zeros_like(bias_s)
        bias_s[0, pl.ds(0, 2), pl.ds(0, DH)] = bias_u[...]
        bias_s[1, pl.ds(0, 2), pl.ds(0, DH)] = bias_v[...]
        for c in range(2):
            gp[c, pl.ds(0, 16), :] = jnp.zeros((16, 128), F32)
            gp[c, pl.ds(16 + FRAMES, 16), :] = jnp.zeros((16, 128), F32)
        odd = jnp.full((1, 256), xh, jnp.int32) == 1
        window = pl.ds(pl.multiple_of((3 * me) // 2 * 128, 128), 256)

        def mine(ref, count):
            part = ref[:, window]
            moved = pltpu.roll(part, 192, 1)
            return jnp.where(jnp.broadcast_to(odd, (count, 256)), moved, part)

        taps = mine(taps_ref, TAPS)
        scale, shift = mine(scale_ref, 1), mine(shift_ref, 1)
        for c in range(2):
            cols = slice(c * 128, c * 128 + 128)
            taps_s[c, pl.ds(0, TAPS), :] = taps[:, cols]
            bn_s[0, pl.ds(c, 1), :] = scale[:, cols]
            bn_s[1, pl.ds(c, 1), :] = shift[:, cols]

    loads[0].wait()
    first_norm(0)
    pl.semaphore_wait(barrier, PEERS - 1 + 3)
    ag_first(0, nrm, 0)
    loads[2].wait()
    wo_start(*range(7))
    loads[1].wait()
    first_norm(1)
    prepare()
    ag_second(0, nrm, 0)
    ag_first(0, nrm, 1)
    ag_third(0, nrm, 0)
    wo_wait(*range(7))
    wo_start(7, 8, 11)
    ag_finish(0, nrm, 0)
    for load in loads[3:]:
        load.wait()
    project(0)
    ag_second(0, nrm, 1)
    attend(0)
    aa_start(0, hs, hb, 0)
    ag_third(0, nrm, 1)
    wo_wait(7)
    wo_start(9, 12)
    wo_wait(8)
    wo_start(10, 13)
    ag_finish(0, nrm, 1)
    project(1)
    attend(1)
    aa_start(0, hs, hb, 1)
    wo_wait(9, 10)
    wo_start(14, 15)
    aa_wait(0, hs, hb, 0)
    wo_wait(*range(11, 16))
    out_project(0)
    ag_first(1, n2, 0)
    aa_wait(0, hs, hb, 1)
    out_project(1)
    ag_second(1, n2, 0)
    ag_first(1, n2, 1)
    ag_third(1, n2, 0)
    ag_finish(1, n2, 0)
    ag_second(1, n2, 1)
    glu(0)
    conv(0)
    aa_start(1, cs, cb, 0)
    ag_third(1, n2, 1)
    ag_finish(1, n2, 1)
    glu(1)
    conv(1)
    aa_start(1, cs, cb, 1)
    aa_wait(1, cs, cb, 0)
    conv_finish(0)
    aa_wait(1, cs, cb, 1)
    conv_finish(1)

    for index in range(16):
        wo_copy(index).wait_send()
    for r in range(2):
        for index in range(9):
            ag(0, nrm, r, index).wait_send()
            ag(1, n2, r, index).wait_send()
        for step in range(1, PEERS):
            aa(0, hs, hb, r, step).wait_send()
            aa(1, cs, cb, r, step).wait_send()


def on_device(
    frames_in, lengths, ln1_gain, w_qkv, bias_u, bias_v, pos_keys, w_out, ln2_gain, w_glu,
    depth_kernel, bn_scale, bn_shift,
):
    any_space, vmem = pl.BlockSpec(memory_space=pl.ANY), pl.BlockSpec(memory_space=pltpu.VMEM)
    smem = pl.BlockSpec(memory_space=pltpu.SMEM)
    gathered = pltpu.VMEM((2, PEERS, FD, D), BF16)
    exchanged = pltpu.VMEM((2, PEERS, FD, CH), BF16)
    dma = pltpu.SemaphoreType.DMA
    return pl.pallas_call(
        kernel,
        out_shape=[jax.ShapeDtypeStruct(frames_in.shape, BF16)] * 2,
        in_specs=[
            any_space, smem, vmem, any_space, vmem, vmem, any_space, any_space, vmem, any_space,
            vmem, vmem, vmem,
        ],
        out_specs=[vmem, vmem],
        scratch_shapes=[
            pltpu.VMEM((2, FD, D), BF16),
            gathered,
            gathered,
            pltpu.VMEM((768, D), BF16),
            pltpu.VMEM((512, D), BF16),
            pltpu.VMEM((PEERS, CH, D), BF16),
            pltpu.VMEM((2, 128, 2 * FRAMES), BF16),
            pltpu.VMEM((FRAMES, 768), BF16),
            pltpu.VMEM((2, FRAMES, 256), BF16),
            exchanged,
            exchanged,
            pltpu.VMEM((2, FRAMES + 32, 128), F32),
            exchanged,
            exchanged,
            pltpu.VMEM((2, 8, 128), F32),
            pltpu.VMEM((2, 32, 128), F32),
            pltpu.VMEM((2, 8, 128), F32),
            dma((12,)),
            dma((2, 2, 9)),
            dma((2, 2, 9)),
            dma((2, 2, PEERS)),
            dma((2, 2, PEERS)),
            dma((16,)),
            dma((16,)),
        ],
        compiler_params=pltpu.CompilerParams(
            collective_id=0, has_side_effects=True, vmem_limit_bytes=48 << 20
        ),
    )(
        frames_in, lengths, ln1_gain.reshape(1, D), w_qkv, bias_u, bias_v, pos_keys, w_out,
        ln2_gain.reshape(1, D), w_glu, depth_kernel, bn_scale.reshape(1, D),
        bn_shift.reshape(1, D),
    )


def solution(mesh):
    placed = (
        P("rec", "tm", None),
        P("rec"),
        P(),
        P(None, "tm", None),
        P("tm", None),
        P("tm", None),
        P("tm", None),
        P("tm", None),
        P(),
        P(None, "tm", None),
        P(),
        P(),
        P(),
    )
    return jax.shard_map(
        on_device,
        mesh=mesh,
        in_specs=placed,
        out_specs=(P("rec", "tm", None), P("rec", "tm", None)),
        check_vma=False,
    )
```

```python
import functools
import math

import jax
import jax.numpy as jnp
from jax import lax
from jax.experimental import pallas as pl
from jax.experimental.pallas import tpu as pltpu
from jax.sharding import PartitionSpec as P

MESH = pl.DeviceIdType.MESH
F32, BF16 = jnp.float32, jnp.bfloat16
PEERS = 8
Z_CHIPS = 8
FD = 64
FRAMES = 512
D = 1536
CH = 192
DH = 96
TAPS = 31
NT = (((1,), (1,)), ((), ()))
NN = (((1,), (0,)), ((), ()))
SCALE2 = math.log2(math.e) / math.sqrt(DH)


def dot(a, b, dims=NN):
    return lax.dot_general(a, b, dims, preferred_element_type=F32)


def norm_rows(values, gain):
    mean = jnp.mean(values, axis=-1, keepdims=True)
    centered = values - mean
    variance = jnp.mean(centered * centered, axis=-1, keepdims=True)
    return (centered * lax.rsqrt(variance + 1e-05) * gain).astype(BF16)


def sigmoid(v):
    return 1.0 / (1.0 + jnp.exp(-v))


def kernel(
    frames_hbm, lengths_hbm, gain1_hbm, w_qkv_hbm, bias_u_hbm, bias_v_hbm, pos_hbm, w_out_hbm,
    gain2_hbm, w_glu_hbm, taps_hbm, scale_hbm, shift_hbm,
    attended, conv_out,
    x, nrm, n2, wq, wg, wo, pos, qkv, vext, hs, hb, gp, cs, cb, bias_s, taps_s, bn_s,
    lengths, gain1, bias_u, bias_v, gain2, taps_ref, scale_ref, shift_ref,
    local_sem, ag_send, ag_recv, aa_send, aa_recv, wo_send, wo_recv,
):
    rec, me = lax.axis_index("rec"), lax.axis_index("tm")
    y, xh = me // 2, lax.rem(me, 2)
    core, z = lax.rem(rec, 2), lax.rem(rec // 2, Z_CHIPS)
    x_lo = rec // (2 * Z_CHIPS)

    def rec_of(zz, cc):
        return (x_lo * Z_CHIPS + lax.rem(zz + Z_CHIPS, Z_CHIPS)) * 2 + cc

    def slot(dy, flip):
        return lax.rem(y + dy, 4) * 2 + (1 - xh if flip else xh)

    s_x, s_up, s_dn, s_far = slot(0, True), slot(1, False), slot(3, False), slot(2, False)
    s_upx, s_dnx, s_farx = slot(1, True), slot(3, True), slot(2, True)
    z_up, z_dn, sibling = rec_of(z + 1, core), rec_of(z - 1, core), rec_of(z, 1 - core)

    def remote(src, dst, send, recv, device):
        return pltpu.make_async_remote_copy(
            src_ref=src, dst_ref=dst, send_sem=send, recv_sem=recv, device_id=device,
            device_id_type=MESH,
        )

    quarter = lax.rem(z, 4)
    wo_rows = pl.ds(pl.multiple_of(quarter * 48, 16), 48)
    wo_cols = pl.ds(pl.multiple_of(core * 768, 128), 768)
    loads = [
        (frames_hbm.at[0], x.at[0]),
        (frames_hbm.at[1], x.at[1]),
        (gain1_hbm, gain1),
        (w_out_hbm.at[wo_rows, wo_cols], wo.at[me, wo_rows, wo_cols]),
        (w_qkv_hbm.at[0, pl.ds(0, DH)], wq.at[pl.ds(0, DH)]),
        (w_qkv_hbm.at[0, pl.ds(DH, DH)], wq.at[pl.ds(128, DH)]),
        (w_qkv_hbm.at[1, pl.ds(0, DH)], wq.at[pl.ds(256, DH)]),
        (w_qkv_hbm.at[1, pl.ds(DH, DH)], wq.at[pl.ds(384, DH)]),
        (w_qkv_hbm.at[2], wq.at[pl.ds(512, CH)]),
        (pos_hbm.at[pl.ds(0, DH)], pos.at[0, pl.ds(0, DH)]),
        (pos_hbm.at[pl.ds(DH, DH)], pos.at[1, pl.ds(0, DH)]),
        (w_glu_hbm.at[0], wg.at[pl.ds(0, CH)]),
        (w_glu_hbm.at[1], wg.at[pl.ds(256, CH)]),
        (lengths_hbm, lengths),
        (bias_u_hbm, bias_u),
        (bias_v_hbm, bias_v),
        (gain2_hbm, gain2),
        (taps_hbm, taps_ref),
        (scale_hbm, scale_ref),
        (shift_hbm, shift_ref),
    ]
    loads = [pltpu.make_async_copy(s, d, local_sem.at[i]) for i, (s, d) in enumerate(loads)]
    for load in loads:
        load.start()

    barrier = pltpu.get_barrier_semaphore()
    for step in range(1, PEERS):
        pl.semaphore_signal(
            barrier, inc=1, device_id=(rec, lax.rem(me + step, PEERS)), device_id_type=MESH
        )
    for other in (z_up, z_dn, sibling):
        pl.semaphore_signal(barrier, inc=1, device_id=(other, me), device_id_type=MESH)

    def ag(which, buf, unit, index, arriving=False):
        plan = [
            (me, 0, s_x, s_x),
            (me, 0, s_up, s_dn),
            (me, 0, s_dn, s_up),
            (s_x, 0, s_up, s_dnx),
            (s_x, 0, s_dn, s_upx),
            (s_dn, 1, s_up, s_far),
            (s_up, 2, s_dn, s_far),
            (s_far, 1, s_x, s_farx),
            (s_far, 2, s_x, s_farx),
        ]
        src, part, target, landing = plan[index]
        rows = pl.ds(unit % 2 * 32 + (16 if part == 2 else 0), 16 if part else 32)
        frames = buf.at[unit // 2, landing if arriving else src, rows]
        sems = (ag_send.at[which, unit, index], ag_recv.at[which, unit, index])
        return remote(frames, frames, *sems, (rec, target))

    def ag_start(which, buf, unit, *indices):
        for index in indices:
            ag(which, buf, unit, index).start()

    def ag_wait(which, buf, unit, *indices):
        for index in indices:
            ag(which, buf, unit, index, True).wait_recv()

    def ag_first(which, buf, *units):
        for unit in units:
            ag_start(which, buf, unit, 0, 1, 2)

    def ag_second(which, buf, *units):
        for unit in units:
            ag_wait(which, buf, unit, 1)
            ag_start(which, buf, unit, 5)
            ag_wait(which, buf, unit, 2)
            ag_start(which, buf, unit, 6)
            ag_wait(which, buf, unit, 0)
            ag_start(which, buf, unit, 3, 4)

    def ag_third(which, buf, *units):
        for unit in units:
            ag_wait(which, buf, unit, 5)
            ag_start(which, buf, unit, 7)
            ag_wait(which, buf, unit, 6)
            ag_start(which, buf, unit, 8)

    def ag_finish(which, buf, *units):
        for unit in units:
            ag_wait(which, buf, unit, 3, 4, 7, 8)

    def aa(which, out, into, r, step, arriving=False):
        to, source = lax.rem(me + step, PEERS), lax.rem(me + PEERS - step, PEERS)
        sems = (aa_send.at[which, r, step], aa_recv.at[which, r, step])
        return remote(out.at[r, to], into.at[r, source if arriving else me], *sems, (rec, to))

    def aa_start(which, out, into, r, step):
        aa(which, out, into, r, step).start()

    def aa_wait(which, out, into, r):
        for step in range(1, PEERS):
            aa(which, out, into, r, step, True).wait_recv()

    def wo_set(q, c, half=None):
        width = 768 if half is None else 384
        start = c * 768 + (0 if half is None else half * 384)
        return wo.at[
            :,
            pl.ds(pl.multiple_of(lax.rem(q + 4, 4) * 48, 16), 48),
            pl.ds(pl.multiple_of(start, 128), width),
        ]

    def wo_copy(index, arriving=False):
        sems = (wo_send.at[index], wo_recv.at[index])
        if index < 7:
            step = index + 1
            to, source = lax.rem(me + step, PEERS), lax.rem(me + PEERS - step, PEERS)
            mine = wo.at[me, wo_rows, wo_cols]
            landed = wo.at[source, wo_rows, wo_cols]
            device = (rec, to)
        elif index < 11:
            q_sent, half, q_land, to = [
                (quarter, None, quarter - 1, z_up),
                (quarter, None, quarter + 1, z_dn),
                (quarter - 1, 0, quarter - 2, z_up),
                (quarter + 1, 1, quarter + 2, z_dn),
            ][index - 7]
            mine, landed = wo_set(q_sent, core, half), wo_set(q_land, core, half)
            device = (to, me)
        else:
            q, half = [
                (quarter, None), (quarter - 1, None), (quarter + 1, None),
                (quarter - 2, 0), (quarter + 2, 1),
            ][index - 11]
            mine, landed = wo_set(q, core, half), wo_set(q, 1 - core, half)
            device = (sibling, me)
        part = landed if arriving else mine
        return remote(part, part, *sems, device)

    def wo_start(*indices):
        for index in indices:
            wo_copy(index).start()

    def wo_wait(*indices):
        for index in indices:
            wo_copy(index, True).wait_recv()

    def first_norm(r):
        nrm[r, me] = norm_rows(x[r].astype(F32), gain1[...].reshape(1, D))

    def project(r):
        rows = nrm.at[r]

        @pl.loop(0, 3)
        def _(n):
            cols = pl.ds(pl.multiple_of(n * 256, 256), 256)
            part = dot(rows[...].reshape(FRAMES, D), wq[cols, :], NT)
            qkv[:, cols] = part.astype(BF16)

        v = qkv[:, pl.ds(512, 256)].astype(F32)
        lane = lax.broadcasted_iota(jnp.int32, v.shape, 1)
        ones = jnp.where(lane == CH, 1.0, 0.0)
        vext[0] = jnp.where(lane < DH, v, ones).astype(BF16)
        vext[1] = jnp.where((lane >= DH) & (lane < CH), v, ones).astype(BF16)

    def attend(r):
        valid = lax.broadcasted_iota(jnp.int32, (128, FRAMES), 1) < lengths[r]

        @pl.loop(1, 5)
        def _(turn):
            block = lax.rem(y + turn, 4)
            mixed = []
            for h in range(2):
                q = qkv[pl.ds(pl.multiple_of(block * 128, 128), 128), pl.ds(h * 128, 128)].astype(F32)
                query_u = (q + bias_s[0, pl.ds(h, 1), :]).astype(BF16)
                query_v = (q + bias_s[1, pl.ds(h, 1), :]).astype(BF16)
                content = dot(query_u, qkv[:, pl.ds(256 + h * 128, 128)], NT)
                window = pos[h, :, pl.ds(pl.multiple_of(384 - block * 128, 128), 640)]
                relative = dot(query_v, window)
                relative = pltpu.roll(relative, 513, 1, stride=1, stride_axis=0)[:, :FRAMES]
                scores = jnp.where(valid, content + relative, -1e30)
                peak = jnp.max(scores, axis=-1, keepdims=True)
                expd = jnp.exp2((scores - peak) * SCALE2).astype(BF16)
                out = dot(expd, vext[h])
                mixed.append(out / out[:, CH : CH + 1])
            lane = lax.broadcasted_iota(jnp.int32, mixed[0].shape, 1)
            both = jnp.where(lane < DH, mixed[0], mixed[1])[:, :CH].astype(BF16)
            hs[r, 2 * block] = both[:FD]
            hs[r, 2 * block + 1] = both[FD:]
            for to in (2 * block, 2 * block + 1):
                step = lax.rem(to - me + PEERS, PEERS)

                @pl.when(step != 0)
                def _():
                    aa_start(0, hs, hb, r, step)

        hb[r, me] = hs[r, me]

    def out_project(r):
        heads = jnp.concatenate([hb[r, s] for s in range(PEERS)], axis=-1)
        for n in range(3):
            cols = pl.ds(n * 512, 512)
            part = dot(heads, wo[:, :, cols].reshape(D, 512))
            attended[r, :, cols] = (x[r, :, cols].astype(F32) + part).astype(BF16)
        n2[r, me] = norm_rows(attended[r].astype(F32), gain2[...].reshape(1, D))

    def glu(r):
        @pl.loop(0, 4)
        def _(block):
            rows = n2[r, pl.ds(block * 2, 2)].reshape(128, D)
            both = dot(rows, wg[...], NT)
            gated = both[:, :256] * sigmoid(both[:, 256:])
            frame = block * 128 + lax.broadcasted_iota(jnp.int32, gated.shape, 0)
            gated = jnp.where(frame < lengths[r], gated, 0.0).astype(BF16).astype(F32)
            at = pl.ds(pl.multiple_of(16 + block * 128, 16), 128)
            gp[0, at, :] = gated[:, :128]
            gp[1, at, :] = gated[:, 128:]

    def conv_block(r, block):
        for c in range(2):
            total = jnp.zeros((FD, 128), F32)
            for t in range(TAPS):
                total += gp[c, pl.ds(block * FD + t + 1, FD), :] * taps_s[c, pl.ds(t, 1), :]
            s = total * bn_s[0, pl.ds(c, 1), :] + bn_s[1, pl.ds(c, 1), :]
            out = (s * sigmoid(s)).astype(BF16)
            if c == 0:
                cs[r, block, :, pl.ds(0, 128)] = out
            else:
                cs[r, block, :, pl.ds(128, 64)] = out[:, :64]

    def conv(r):
        @pl.loop(1, PEERS)
        def _(step):
            conv_block(r, lax.rem(me + step, PEERS))
            aa_start(1, cs, cb, r, step)

        conv_block(r, me)
        cb[r, me] = cs[r, me]

    def conv_finish(r):
        conv_out[r] = jnp.concatenate([cb[r, s] for s in range(PEERS)], axis=-1)

    def prepare():
        for start in (96, 224, 352, 480):
            wq[pl.ds(start, 32), :] = jnp.zeros((32, D), BF16)
        wq[pl.ds(704, 64), :] = jnp.zeros((64, D), BF16)
        for start in (192, 448):
            wg[pl.ds(start, 64), :] = jnp.zeros((64, D), BF16)
        for h in range(2):
            pos[h, pl.ds(DH, 32), :] = jnp.zeros((32, 2 * FRAMES), BF16)
        bias_s[...] = jnp.zeros_like(bias_s)
        bias_s[0, pl.ds(0, 2), pl.ds(0, DH)] = bias_u[...]
        bias_s[1, pl.ds(0, 2), pl.ds(0, DH)] = bias_v[...]
        for c in range(2):
            gp[c, pl.ds(0, 16), :] = jnp.zeros((16, 128), F32)
            gp[c, pl.ds(16 + FRAMES, 16), :] = jnp.zeros((16, 128), F32)
        odd = jnp.full((1, 256), xh, jnp.int32) == 1
        window = pl.ds(pl.multiple_of((3 * me) // 2 * 128, 128), 256)

        def mine(ref, count):
            part = ref[:, window] if count > 1 else ref[window].reshape(1, 256)
            moved = pltpu.roll(part, 192, 1)
            return jnp.where(jnp.broadcast_to(odd, (count, 256)), moved, part)

        taps = mine(taps_ref, TAPS)
        scale, shift = mine(scale_ref, 1), mine(shift_ref, 1)
        for c in range(2):
            cols = slice(c * 128, c * 128 + 128)
            taps_s[c, pl.ds(0, TAPS), :] = taps[:, cols]
            bn_s[0, pl.ds(c, 1), :] = scale[:, cols]
            bn_s[1, pl.ds(c, 1), :] = shift[:, cols]

    loads[0].wait()
    loads[2].wait()
    first_norm(0)
    pl.semaphore_wait(barrier, PEERS - 1 + 3)
    ag_first(0, nrm, 0, 1)
    loads[1].wait()
    first_norm(1)
    ag_first(0, nrm, 2, 3)
    loads[3].wait()
    wo_start(*range(7))
    for load in loads[4:]:
        load.wait()
    prepare()
    ag_second(0, nrm, 0, 1)
    ag_third(0, nrm, 0)
    ag_second(0, nrm, 2)
    ag_third(0, nrm, 1)
    ag_second(0, nrm, 3)
    wo_wait(*range(7))
    wo_start(7, 8, 11)
    ag_third(0, nrm, 2)
    ag_finish(0, nrm, 0, 1)
    project(0)
    ag_third(0, nrm, 3)
    attend(0)
    ag_finish(0, nrm, 2, 3)
    project(1)
    wo_wait(7)
    wo_start(9, 12)
    wo_wait(8)
    wo_start(10, 13)
    attend(1)
    wo_wait(9, 10)
    wo_start(14, 15)
    aa_wait(0, hs, hb, 0)
    wo_wait(*range(11, 16))
    out_project(0)
    ag_first(1, n2, 0, 1)
    aa_wait(0, hs, hb, 1)
    out_project(1)
    ag_first(1, n2, 2, 3)
    ag_second(1, n2, 0, 1)
    ag_third(1, n2, 0)
    ag_second(1, n2, 2)
    ag_third(1, n2, 1)
    ag_second(1, n2, 3)
    ag_third(1, n2, 2)
    ag_finish(1, n2, 0, 1)
    glu(0)
    ag_third(1, n2, 3)
    conv(0)
    ag_finish(1, n2, 2, 3)
    glu(1)
    conv(1)
    aa_wait(1, cs, cb, 0)
    conv_finish(0)
    aa_wait(1, cs, cb, 1)
    conv_finish(1)

    for index in range(16):
        wo_copy(index).wait_send()
    for unit in range(4):
        for index in range(9):
            ag(0, nrm, unit, index).wait_send()
            ag(1, n2, unit, index).wait_send()
    for r in range(2):
        for step in range(1, PEERS):
            aa(0, hs, hb, r, step).wait_send()
            aa(1, cs, cb, r, step).wait_send()


def on_device(
    frames_in, lengths, ln1_gain, w_qkv, bias_u, bias_v, pos_keys, w_out, ln2_gain, w_glu,
    depth_kernel, bn_scale, bn_shift,
):
    vmem = pl.BlockSpec(memory_space=pltpu.VMEM)
    gathered = pltpu.VMEM((2, PEERS, FD, D), BF16)
    exchanged = pltpu.VMEM((2, PEERS, FD, CH), BF16)
    dma = pltpu.SemaphoreType.DMA
    return pl.pallas_call(
        kernel,
        out_shape=[jax.ShapeDtypeStruct(frames_in.shape, BF16)] * 2,
        in_specs=[pl.BlockSpec(memory_space=pl.ANY)] * 13,
        out_specs=[vmem, vmem],
        scratch_shapes=[
            pltpu.VMEM((2, FD, D), BF16),
            gathered,
            gathered,
            pltpu.VMEM((768, D), BF16),
            pltpu.VMEM((512, D), BF16),
            pltpu.VMEM((PEERS, CH, D), BF16),
            pltpu.VMEM((2, 128, 2 * FRAMES), BF16),
            pltpu.VMEM((FRAMES, 768), BF16),
            pltpu.VMEM((2, FRAMES, 256), BF16),
            exchanged,
            exchanged,
            pltpu.VMEM((2, FRAMES + 32, 128), F32),
            exchanged,
            exchanged,
            pltpu.VMEM((2, 8, 128), F32),
            pltpu.VMEM((2, 32, 128), F32),
            pltpu.VMEM((2, 8, 128), F32),
            pltpu.SMEM((2,), jnp.int32),
            pltpu.VMEM((D,), F32),
            pltpu.VMEM((2, DH), F32),
            pltpu.VMEM((2, DH), F32),
            pltpu.VMEM((D,), F32),
            pltpu.VMEM((TAPS, D), F32),
            pltpu.VMEM((D,), F32),
            pltpu.VMEM((D,), F32),
            dma((20,)),
            dma((2, 4, 9)),
            dma((2, 4, 9)),
            dma((2, 2, PEERS)),
            dma((2, 2, PEERS)),
            dma((16,)),
            dma((16,)),
        ],
        compiler_params=pltpu.CompilerParams(
            collective_id=0, has_side_effects=True, vmem_limit_bytes=60 << 20
        ),
    )(
        frames_in, lengths, ln1_gain, w_qkv, bias_u, bias_v, pos_keys, w_out, ln2_gain, w_glu,
        depth_kernel, bn_scale, bn_shift,
    )


def solution(mesh):
    placed = (
        P("rec", "tm", None),
        P("rec"),
        P(),
        P(None, "tm", None),
        P("tm", None),
        P("tm", None),
        P("tm", None),
        P("tm", None),
        P(),
        P(None, "tm", None),
        P(),
        P(),
        P(),
    )
    return jax.shard_map(
        on_device,
        mesh=mesh,
        in_specs=placed,
        out_specs=(P("rec", "tm", None), P("rec", "tm", None)),
        check_vma=False,
    )
```

```python
import functools
import math

import jax
import jax.numpy as jnp
from jax import lax
from jax.experimental import pallas as pl
from jax.experimental.pallas import tpu as pltpu
from jax.sharding import PartitionSpec as P

MESH = pl.DeviceIdType.MESH
F32, BF16 = jnp.float32, jnp.bfloat16
PEERS = 8
Z_CHIPS = 8
FD = 64
FRAMES = 512
D = 1536
CH = 192
DH = 96
TAPS = 31
NT = (((1,), (1,)), ((), ()))
NN = (((1,), (0,)), ((), ()))
SCALE2 = math.log2(math.e) / math.sqrt(DH)


def dot(a, b, dims=NN):
    return lax.dot_general(a, b, dims, preferred_element_type=F32)


def norm_rows(values, gain):
    mean = jnp.mean(values, axis=-1, keepdims=True)
    centered = values - mean
    variance = jnp.mean(centered * centered, axis=-1, keepdims=True)
    return (centered * lax.rsqrt(variance + 1e-05) * gain).astype(BF16)


def sigmoid(v):
    return 1.0 / (1.0 + jnp.exp(-v))


def kernel(
    frames_hbm, lengths_hbm, gain1_hbm, w_qkv_hbm, bias_u_hbm, bias_v_hbm, pos_hbm, w_out_hbm,
    gain2_hbm, w_glu_hbm, taps_hbm, scale_hbm, shift_hbm,
    attended, conv_out,
    x, nrm, n2, wq, wg, wo, pos, qkv, vext, hs, hb, gp, cs, cb, bias_s, taps_s, bn_s,
    lengths, gain1, bias_u, bias_v, gain2, taps_ref, scale_ref, shift_ref,
    local_sem, ag_send, ag_recv, aa_send, aa_recv, wo_send, wo_recv,
):
    rec, me = lax.axis_index("rec"), lax.axis_index("tm")
    y, xh = me // 2, lax.rem(me, 2)
    core, z = lax.rem(rec, 2), lax.rem(rec // 2, Z_CHIPS)
    x_lo = rec // (2 * Z_CHIPS)

    def rec_of(zz, cc):
        return (x_lo * Z_CHIPS + lax.rem(zz + Z_CHIPS, Z_CHIPS)) * 2 + cc

    def slot(dy, flip):
        return lax.rem(y + dy, 4) * 2 + (1 - xh if flip else xh)

    s_x, s_up, s_dn, s_far = slot(0, True), slot(1, False), slot(3, False), slot(2, False)
    s_upx, s_dnx, s_farx = slot(1, True), slot(3, True), slot(2, True)
    z_up, z_dn, sibling = rec_of(z + 1, core), rec_of(z - 1, core), rec_of(z, 1 - core)

    def remote(src, dst, send, recv, device):
        return pltpu.make_async_remote_copy(
            src_ref=src, dst_ref=dst, send_sem=send, recv_sem=recv, device_id=device,
            device_id_type=MESH,
        )

    quarter = lax.rem(z, 4)
    wo_rows = pl.ds(pl.multiple_of(quarter * 48, 16), 48)
    wo_cols = pl.ds(pl.multiple_of(core * 768, 128), 768)
    loads = [
        (frames_hbm.at[0], x.at[0]),
        (frames_hbm.at[1], x.at[1]),
        (gain1_hbm, gain1),
        (w_out_hbm.at[wo_rows, wo_cols], wo.at[me, wo_rows, wo_cols]),
        (w_qkv_hbm.at[0, pl.ds(0, DH)], wq.at[pl.ds(0, DH)]),
        (w_qkv_hbm.at[0, pl.ds(DH, DH)], wq.at[pl.ds(128, DH)]),
        (w_qkv_hbm.at[1, pl.ds(0, DH)], wq.at[pl.ds(256, DH)]),
        (w_qkv_hbm.at[1, pl.ds(DH, DH)], wq.at[pl.ds(384, DH)]),
        (w_qkv_hbm.at[2], wq.at[pl.ds(512, CH)]),
        (pos_hbm.at[pl.ds(0, DH)], pos.at[0, pl.ds(0, DH)]),
        (pos_hbm.at[pl.ds(DH, DH)], pos.at[1, pl.ds(0, DH)]),
        (w_glu_hbm.at[0, pl.ds(0, 128)], wg.at[pl.ds(0, 128)]),
        (w_glu_hbm.at[1, pl.ds(0, 128)], wg.at[pl.ds(128, 128)]),
        (w_glu_hbm.at[0, pl.ds(128, 64)], wg.at[pl.ds(256, 64)]),
        (w_glu_hbm.at[1, pl.ds(128, 64)], wg.at[pl.ds(384, 64)]),
        (lengths_hbm, lengths),
        (bias_u_hbm, bias_u),
        (bias_v_hbm, bias_v),
        (gain2_hbm, gain2),
        (taps_hbm, taps_ref),
        (scale_hbm, scale_ref),
        (shift_hbm, shift_ref),
    ]
    loads = [pltpu.make_async_copy(s, d, local_sem.at[i]) for i, (s, d) in enumerate(loads)]
    for load in loads:
        load.start()

    barrier = pltpu.get_barrier_semaphore()
    for step in range(1, PEERS):
        pl.semaphore_signal(
            barrier, inc=1, device_id=(rec, lax.rem(me + step, PEERS)), device_id_type=MESH
        )
    for other in (z_up, z_dn, sibling):
        pl.semaphore_signal(barrier, inc=1, device_id=(other, me), device_id_type=MESH)

    def ag(which, buf, unit, index, arriving=False):
        plan = [
            (me, 0, s_x, s_x),
            (me, 0, s_up, s_dn),
            (me, 0, s_dn, s_up),
            (s_x, 0, s_up, s_dnx),
            (s_x, 0, s_dn, s_upx),
            (s_dn, 1, s_up, s_far),
            (s_up, 2, s_dn, s_far),
            (s_far, 1, s_x, s_farx),
            (s_far, 2, s_x, s_farx),
        ]
        src, part, target, landing = plan[index]
        rows = pl.ds(unit % 2 * 32 + (16 if part == 2 else 0), 16 if part else 32)
        frames = buf.at[unit // 2, landing if arriving else src, rows]
        sems = (ag_send.at[which, unit, index], ag_recv.at[which, unit, index])
        return remote(frames, frames, *sems, (rec, target))

    def ag_start(which, buf, unit, *indices):
        for index in indices:
            ag(which, buf, unit, index).start()

    def ag_wait(which, buf, unit, *indices):
        for index in indices:
            ag(which, buf, unit, index, True).wait_recv()

    def ag_first(which, buf, *units):
        for unit in units:
            ag_start(which, buf, unit, 0, 1, 2)

    def ag_second(which, buf, *units):
        for unit in units:
            ag_wait(which, buf, unit, 1)
            ag_start(which, buf, unit, 5)
            ag_wait(which, buf, unit, 2)
            ag_start(which, buf, unit, 6)
            ag_wait(which, buf, unit, 0)
            ag_start(which, buf, unit, 3, 4)

    def ag_third(which, buf, *units):
        for unit in units:
            ag_wait(which, buf, unit, 5)
            ag_start(which, buf, unit, 7)
            ag_wait(which, buf, unit, 6)
            ag_start(which, buf, unit, 8)

    def ag_finish(which, buf, *units):
        for unit in units:
            ag_wait(which, buf, unit, 3, 4, 7, 8)

    def aa(which, out, into, r, step, arriving=False):
        to, source = lax.rem(me + step, PEERS), lax.rem(me + PEERS - step, PEERS)
        sems = (aa_send.at[which, r, step], aa_recv.at[which, r, step])
        return remote(out.at[r, to], into.at[r, source if arriving else me], *sems, (rec, to))

    def aa_start(which, out, into, r, step):
        aa(which, out, into, r, step).start()

    def aa_wait(which, out, into, r):
        for step in range(1, PEERS):
            aa(which, out, into, r, step, True).wait_recv()

    def wo_set(q, c, half=None):
        width = 768 if half is None else 384
        start = c * 768 + (0 if half is None else half * 384)
        return wo.at[
            :,
            pl.ds(pl.multiple_of(lax.rem(q + 4, 4) * 48, 16), 48),
            pl.ds(pl.multiple_of(start, 128), width),
        ]

    def wo_copy(index, arriving=False):
        sems = (wo_send.at[index], wo_recv.at[index])
        if index < 7:
            step = index + 1
            to, source = lax.rem(me + step, PEERS), lax.rem(me + PEERS - step, PEERS)
            mine = wo.at[me, wo_rows, wo_cols]
            landed = wo.at[source, wo_rows, wo_cols]
            device = (rec, to)
        elif index < 11:
            q_sent, half, q_land, to = [
                (quarter, None, quarter - 1, z_up),
                (quarter, None, quarter + 1, z_dn),
                (quarter - 1, 0, quarter - 2, z_up),
                (quarter + 1, 1, quarter + 2, z_dn),
            ][index - 7]
            mine, landed = wo_set(q_sent, core, half), wo_set(q_land, core, half)
            device = (to, me)
        else:
            q, half = [
                (quarter, None), (quarter - 1, None), (quarter + 1, None),
                (quarter - 2, 0), (quarter + 2, 1),
            ][index - 11]
            mine, landed = wo_set(q, core, half), wo_set(q, 1 - core, half)
            device = (sibling, me)
        part = landed if arriving else mine
        return remote(part, part, *sems, device)

    def wo_start(*indices):
        for index in indices:
            wo_copy(index).start()

    def wo_wait(*indices):
        for index in indices:
            wo_copy(index, True).wait_recv()

    def first_norm(r):
        nrm[r, me] = norm_rows(x[r].astype(F32), gain1[...].reshape(1, D))

    def project(unit):
        r, part_rows = unit // 2, pl.ds(unit % 2 * 32, 32)

        @pl.loop(0, 3)
        def _(n):
            cols = pl.ds(pl.multiple_of(n * 256, 256), 256)
            part = dot(nrm[r, :, part_rows, :].reshape(256, D), wq[cols, :], NT)
            qkv[:, part_rows, cols] = part.astype(BF16).reshape(PEERS, 32, 256)

        v = qkv[:, part_rows, pl.ds(512, 256)].astype(F32)
        lane = lax.broadcasted_iota(jnp.int32, v.shape, 2)
        ones = jnp.where(lane == CH, 1.0, 0.0)
        vext[0, :, part_rows, :] = jnp.where(lane < DH, v, ones).astype(BF16)
        vext[1, :, part_rows, :] = jnp.where((lane >= DH) & (lane < CH), v, ones).astype(BF16)

    def attend(r):
        valid = lax.broadcasted_iota(jnp.int32, (128, FRAMES), 1) < lengths[r]

        @pl.loop(1, 5)
        def _(turn):
            block = lax.rem(y + turn, 4)
            mixed = []
            for h in range(2):
                q = qkv[pl.ds(2 * block, 2), :, pl.ds(h * 128, 128)].reshape(128, 128).astype(F32)
                query_u = (q + bias_s[0, pl.ds(h, 1), :]).astype(BF16)
                query_v = (q + bias_s[1, pl.ds(h, 1), :]).astype(BF16)
                keys = qkv[:, :, pl.ds(256 + h * 128, 128)].reshape(FRAMES, 128)
                content = dot(query_u, keys, NT)
                window = pos[h, :, pl.ds(pl.multiple_of(384 - block * 128, 128), 640)]
                relative = dot(query_v, window)
                relative = pltpu.roll(relative, 513, 1, stride=1, stride_axis=0)[:, :FRAMES]
                scores = jnp.where(valid, content + relative, -1e30)
                peak = jnp.max(scores, axis=-1, keepdims=True)
                expd = jnp.exp2((scores - peak) * SCALE2).astype(BF16)
                out = dot(expd, vext[h].reshape(FRAMES, 256))
                mixed.append(out / out[:, CH : CH + 1])
            lane = lax.broadcasted_iota(jnp.int32, mixed[0].shape, 1)
            both = jnp.where(lane < DH, mixed[0], mixed[1])[:, :CH].astype(BF16)
            hs[r, 2 * block] = both[:FD]
            hs[r, 2 * block + 1] = both[FD:]
            for to in (2 * block, 2 * block + 1):
                step = lax.rem(to - me + PEERS, PEERS)

                @pl.when(step != 0)
                def _():
                    aa_start(0, hs, hb, r, step)

        hb[r, me] = hs[r, me]

    def out_project(r):
        heads = jnp.concatenate([hb[r, s] for s in range(PEERS)], axis=-1)
        for n in range(3):
            cols = pl.ds(n * 512, 512)
            part = dot(heads, wo[:, :, cols].reshape(D, 512))
            attended[r, :, cols] = (x[r, :, cols].astype(F32) + part).astype(BF16)
        n2[r, me] = norm_rows(attended[r].astype(F32), gain2[...].reshape(1, D))

    def glu(unit):
        r, start = unit // 2, unit % 2 * 32

        @pl.loop(0, 2)
        def _(c):
            rows = n2[r, :, pl.ds(start, 32), :].reshape(256, D)
            both = dot(rows, wg[pl.ds(pl.multiple_of(c * 256, 256), 256), :], NT)
            gated = (both[:, :128] * sigmoid(both[:, 128:])).reshape(PEERS, 32, 128)
            frame = lax.broadcasted_iota(jnp.int32, gated.shape, 0) * FD
            frame += start + lax.broadcasted_iota(jnp.int32, gated.shape, 1)
            gated = jnp.where(frame < lengths[r], gated, 0.0).astype(BF16).astype(F32)
            for s in range(PEERS):
                gp[c, pl.ds(16 + s * FD + start, 32), :] = gated[s]

    def conv_block(r, block):
        for c in range(2):
            total = jnp.zeros((FD, 128), F32)
            for t in range(TAPS):
                total += gp[c, pl.ds(block * FD + t + 1, FD), :] * taps_s[c, pl.ds(t, 1), :]
            s = total * bn_s[0, pl.ds(c, 1), :] + bn_s[1, pl.ds(c, 1), :]
            out = (s * sigmoid(s)).astype(BF16)
            if c == 0:
                cs[r, block, :, pl.ds(0, 128)] = out
            else:
                cs[r, block, :, pl.ds(128, 64)] = out[:, :64]

    def conv(r):
        @pl.loop(1, PEERS)
        def _(step):
            conv_block(r, lax.rem(me + step, PEERS))
            aa_start(1, cs, cb, r, step)

        conv_block(r, me)
        cb[r, me] = cs[r, me]

    def conv_finish(r):
        conv_out[r] = jnp.concatenate([cb[r, s] for s in range(PEERS)], axis=-1)

    def prepare():
        for start in (96, 224, 352, 480):
            wq[pl.ds(start, 32), :] = jnp.zeros((32, D), BF16)
        wq[pl.ds(704, 64), :] = jnp.zeros((64, D), BF16)
        for start in (320, 448):
            wg[pl.ds(start, 64), :] = jnp.zeros((64, D), BF16)
        for h in range(2):
            pos[h, pl.ds(DH, 32), :] = jnp.zeros((32, 2 * FRAMES), BF16)
        bias_s[...] = jnp.zeros_like(bias_s)
        bias_s[0, pl.ds(0, 2), pl.ds(0, DH)] = bias_u[...]
        bias_s[1, pl.ds(0, 2), pl.ds(0, DH)] = bias_v[...]
        for c in range(2):
            gp[c, pl.ds(0, 16), :] = jnp.zeros((16, 128), F32)
            gp[c, pl.ds(16 + FRAMES, 16), :] = jnp.zeros((16, 128), F32)
        odd = jnp.full((1, 256), xh, jnp.int32) == 1
        window = pl.ds(pl.multiple_of((3 * me) // 2 * 128, 128), 256)

        def mine(ref, count):
            part = ref[:, window] if count > 1 else ref[window].reshape(1, 256)
            moved = pltpu.roll(part, 192, 1)
            return jnp.where(jnp.broadcast_to(odd, (count, 256)), moved, part)

        taps = mine(taps_ref, TAPS)
        scale, shift = mine(scale_ref, 1), mine(shift_ref, 1)
        for c in range(2):
            cols = slice(c * 128, c * 128 + 128)
            taps_s[c, pl.ds(0, TAPS), :] = taps[:, cols]
            bn_s[0, pl.ds(c, 1), :] = scale[:, cols]
            bn_s[1, pl.ds(c, 1), :] = shift[:, cols]

    loads[0].wait()
    loads[2].wait()
    first_norm(0)
    pl.semaphore_wait(barrier, PEERS - 1 + 3)
    ag_first(0, nrm, 0, 1)
    loads[1].wait()
    first_norm(1)
    ag_first(0, nrm, 2, 3)
    loads[3].wait()
    wo_start(*range(7))
    for load in loads[4:]:
        load.wait()
    prepare()
    ag_second(0, nrm, 0, 1)
    ag_third(0, nrm, 0)
    ag_second(0, nrm, 2)
    ag_third(0, nrm, 1)
    ag_second(0, nrm, 3)
    wo_wait(*range(7))
    wo_start(7, 8, 11)
    ag_third(0, nrm, 2)
    ag_finish(0, nrm, 0)
    project(0)
    ag_finish(0, nrm, 1)
    project(1)
    ag_third(0, nrm, 3)
    attend(0)
    ag_finish(0, nrm, 2)
    project(2)
    ag_finish(0, nrm, 3)
    project(3)
    wo_wait(7)
    wo_start(9, 12)
    wo_wait(8)
    wo_start(10, 13)
    attend(1)
    wo_wait(9, 10)
    wo_start(14, 15)
    aa_wait(0, hs, hb, 0)
    wo_wait(*range(11, 16))
    out_project(0)
    ag_first(1, n2, 0, 1)
    aa_wait(0, hs, hb, 1)
    out_project(1)
    ag_first(1, n2, 2, 3)
    ag_second(1, n2, 0, 1)
    ag_third(1, n2, 0)
    ag_second(1, n2, 2)
    ag_third(1, n2, 1)
    ag_second(1, n2, 3)
    ag_third(1, n2, 2)
    ag_finish(1, n2, 0)
    glu(0)
    ag_finish(1, n2, 1)
    glu(1)
    ag_third(1, n2, 3)
    conv(0)
    ag_finish(1, n2, 2)
    glu(2)
    ag_finish(1, n2, 3)
    glu(3)
    conv(1)
    aa_wait(1, cs, cb, 0)
    conv_finish(0)
    aa_wait(1, cs, cb, 1)
    conv_finish(1)

    for index in range(16):
        wo_copy(index).wait_send()
    for unit in range(4):
        for index in range(9):
            ag(0, nrm, unit, index).wait_send()
            ag(1, n2, unit, index).wait_send()
    for r in range(2):
        for step in range(1, PEERS):
            aa(0, hs, hb, r, step).wait_send()
            aa(1, cs, cb, r, step).wait_send()


def on_device(
    frames_in, lengths, ln1_gain, w_qkv, bias_u, bias_v, pos_keys, w_out, ln2_gain, w_glu,
    depth_kernel, bn_scale, bn_shift,
):
    vmem = pl.BlockSpec(memory_space=pltpu.VMEM)
    gathered = pltpu.VMEM((2, PEERS, FD, D), BF16)
    exchanged = pltpu.VMEM((2, PEERS, FD, CH), BF16)
    dma = pltpu.SemaphoreType.DMA
    return pl.pallas_call(
        kernel,
        out_shape=[pltpu.VMEM(frames_in.shape, BF16)] * 2,
        in_specs=[pl.BlockSpec(memory_space=pl.ANY)] * 13,
        out_specs=[vmem, vmem],
        scratch_shapes=[
            pltpu.VMEM((2, FD, D), BF16),
            gathered,
            gathered,
            pltpu.VMEM((768, D), BF16),
            pltpu.VMEM((512, D), BF16),
            pltpu.VMEM((PEERS, CH, D), BF16),
            pltpu.VMEM((2, 128, 2 * FRAMES), BF16),
            pltpu.VMEM((PEERS, FD, 768), BF16),
            pltpu.VMEM((2, PEERS, FD, 256), BF16),
            exchanged,
            exchanged,
            pltpu.VMEM((2, FRAMES + 32, 128), F32),
            exchanged,
            exchanged,
            pltpu.VMEM((2, 8, 128), F32),
            pltpu.VMEM((2, 32, 128), F32),
            pltpu.VMEM((2, 8, 128), F32),
            pltpu.SMEM((2,), jnp.int32),
            pltpu.VMEM((D,), F32),
            pltpu.VMEM((2, DH), F32),
            pltpu.VMEM((2, DH), F32),
            pltpu.VMEM((D,), F32),
            pltpu.VMEM((TAPS, D), F32),
            pltpu.VMEM((D,), F32),
            pltpu.VMEM((D,), F32),
            dma((22,)),
            dma((2, 4, 9)),
            dma((2, 4, 9)),
            dma((2, 2, PEERS)),
            dma((2, 2, PEERS)),
            dma((16,)),
            dma((16,)),
        ],
        compiler_params=pltpu.CompilerParams(
            collective_id=0, has_side_effects=True, vmem_limit_bytes=60 << 20
        ),
    )(
        frames_in, lengths, ln1_gain, w_qkv, bias_u, bias_v, pos_keys, w_out, ln2_gain, w_glu,
        depth_kernel, bn_scale, bn_shift,
    )


def solution(mesh):
    placed = (
        P("rec", "tm", None),
        P("rec"),
        P(),
        P(None, "tm", None),
        P("tm", None),
        P("tm", None),
        P("tm", None),
        P("tm", None),
        P(),
        P(None, "tm", None),
        P(),
        P(),
        P(),
    )
    return jax.shard_map(
        on_device,
        mesh=mesh,
        in_specs=placed,
        out_specs=(P("rec", "tm", None), P("rec", "tm", None)),
        check_vma=False,
    )
```

```python
import functools
import math

import jax
import jax.numpy as jnp
from jax import lax
from jax.experimental import pallas as pl
from jax.experimental.pallas import tpu as pltpu
from jax.sharding import PartitionSpec as P

MESH = pl.DeviceIdType.MESH
F32, BF16 = jnp.float32, jnp.bfloat16
PEERS = 8
Z_CHIPS = 8
FD = 64
FRAMES = 512
D = 1536
CH = 192
DH = 96
TAPS = 31
NT = (((1,), (1,)), ((), ()))
NN = (((1,), (0,)), ((), ()))
SCALE2 = math.log2(math.e) / math.sqrt(DH)


def dot(a, b, dims=NN):
    return lax.dot_general(a, b, dims, preferred_element_type=F32)


def norm_rows(values, gain):
    mean = jnp.mean(values, axis=-1, keepdims=True)
    centered = values - mean
    variance = jnp.mean(centered * centered, axis=-1, keepdims=True)
    return (centered * lax.rsqrt(variance + 1e-05) * gain).astype(BF16)


def sigmoid(v):
    return 1.0 / (1.0 + jnp.exp(-v))


def kernel(
    frames_hbm, lengths_hbm, gain1_hbm, w_qkv_hbm, bias_u_hbm, bias_v_hbm, pos_hbm, w_out_hbm,
    gain2_hbm, w_glu_hbm, taps_hbm, scale_hbm, shift_hbm,
    attended, conv_out,
    x, nrm, n2, wq, wg, wo, pos, qkv, vext, hs, hb, gp, cs, cb, bias_s, taps_s, bn_s,
    lengths, gain1, bias_u, bias_v, gain2, taps_ref, scale_ref, shift_ref,
    local_sem, ag_send, ag_recv, aa_send, aa_recv, wo_send, wo_recv,
):
    rec, me = lax.axis_index("rec"), lax.axis_index("tm")
    y, xh = me // 2, lax.rem(me, 2)
    core, z = lax.rem(rec, 2), lax.rem(rec // 2, Z_CHIPS)
    x_lo = rec // (2 * Z_CHIPS)

    def rec_of(zz, cc):
        return (x_lo * Z_CHIPS + lax.rem(zz + Z_CHIPS, Z_CHIPS)) * 2 + cc

    def slot(dy, flip):
        return lax.rem(y + dy, 4) * 2 + (1 - xh if flip else xh)

    s_x, s_up, s_dn, s_far = slot(0, True), slot(1, False), slot(3, False), slot(2, False)
    s_upx, s_dnx, s_farx = slot(1, True), slot(3, True), slot(2, True)
    z_up, z_dn, sibling = rec_of(z + 1, core), rec_of(z - 1, core), rec_of(z, 1 - core)

    def remote(src, dst, send, recv, device):
        return pltpu.make_async_remote_copy(
            src_ref=src, dst_ref=dst, send_sem=send, recv_sem=recv, device_id=device,
            device_id_type=MESH,
        )

    quarter = lax.rem(z, 4)
    wo_rows = pl.ds(pl.multiple_of(quarter * 48, 16), 48)
    wo_cols = pl.ds(pl.multiple_of(core * 768, 128), 768)
    loads = [
        (frames_hbm.at[0], x.at[0]),
        (frames_hbm.at[1], x.at[1]),
        (gain1_hbm, gain1),
        (w_out_hbm.at[wo_rows, wo_cols], wo.at[me, wo_rows, wo_cols]),
        (w_qkv_hbm.at[0, pl.ds(0, DH)], wq.at[pl.ds(0, DH)]),
        (w_qkv_hbm.at[0, pl.ds(DH, DH)], wq.at[pl.ds(128, DH)]),
        (w_qkv_hbm.at[1, pl.ds(0, DH)], wq.at[pl.ds(256, DH)]),
        (w_qkv_hbm.at[1, pl.ds(DH, DH)], wq.at[pl.ds(384, DH)]),
        (w_qkv_hbm.at[2], wq.at[pl.ds(512, CH)]),
        (pos_hbm.at[pl.ds(0, DH)], pos.at[0, pl.ds(0, DH)]),
        (pos_hbm.at[pl.ds(DH, DH)], pos.at[1, pl.ds(0, DH)]),
        (w_glu_hbm.at[0, pl.ds(0, 128)], wg.at[pl.ds(0, 128)]),
        (w_glu_hbm.at[1, pl.ds(0, 128)], wg.at[pl.ds(128, 128)]),
        (w_glu_hbm.at[0, pl.ds(128, 64)], wg.at[pl.ds(256, 64)]),
        (w_glu_hbm.at[1, pl.ds(128, 64)], wg.at[pl.ds(384, 64)]),
        (lengths_hbm, lengths),
        (bias_u_hbm, bias_u),
        (bias_v_hbm, bias_v),
        (gain2_hbm, gain2),
        (taps_hbm, taps_ref),
        (scale_hbm, scale_ref),
        (shift_hbm, shift_ref),
    ]
    loads = [pltpu.make_async_copy(s, d, local_sem.at[i]) for i, (s, d) in enumerate(loads)]
    for load in loads:
        load.start()

    barrier = pltpu.get_barrier_semaphore()
    for step in range(1, PEERS):
        pl.semaphore_signal(
            barrier, inc=1, device_id=(rec, lax.rem(me + step, PEERS)), device_id_type=MESH
        )
    for other in (z_up, z_dn, sibling):
        pl.semaphore_signal(barrier, inc=1, device_id=(other, me), device_id_type=MESH)

    def ag(which, buf, unit, index, arriving=False):
        plan = [
            (me, 0, s_x, s_x),
            (me, 0, s_up, s_dn),
            (me, 0, s_dn, s_up),
            (s_x, 0, s_up, s_dnx),
            (s_x, 0, s_dn, s_upx),
            (s_dn, 1, s_up, s_far),
            (s_up, 2, s_dn, s_far),
            (s_far, 1, s_x, s_farx),
            (s_far, 2, s_x, s_farx),
        ]
        src, part, target, landing = plan[index]
        rows = pl.ds(unit % 2 * 32 + (16 if part == 2 else 0), 16 if part else 32)
        frames = buf.at[unit // 2, landing if arriving else src, rows]
        sems = (ag_send.at[which, unit, index], ag_recv.at[which, unit, index])
        return remote(frames, frames, *sems, (rec, target))

    def ag_start(which, buf, unit, *indices):
        for index in indices:
            ag(which, buf, unit, index).start()

    def ag_wait(which, buf, unit, *indices):
        for index in indices:
            ag(which, buf, unit, index, True).wait_recv()

    def ag_first(which, buf, *units):
        for unit in units:
            ag_start(which, buf, unit, 0, 1, 2)

    def ag_second(which, buf, *units):
        for unit in units:
            ag_wait(which, buf, unit, 1)
            ag_start(which, buf, unit, 5)
            ag_wait(which, buf, unit, 2)
            ag_start(which, buf, unit, 6)
            ag_wait(which, buf, unit, 0)
            ag_start(which, buf, unit, 3, 4)

    def ag_third(which, buf, *units):
        for unit in units:
            ag_wait(which, buf, unit, 5)
            ag_start(which, buf, unit, 7)
            ag_wait(which, buf, unit, 6)
            ag_start(which, buf, unit, 8)

    def ag_finish(which, buf, *units):
        for unit in units:
            ag_wait(which, buf, unit, 3, 4, 7, 8)

    def aa(which, out, into, r, step, arriving=False):
        to, source = lax.rem(me + step, PEERS), lax.rem(me + PEERS - step, PEERS)
        sems = (aa_send.at[which, r, step], aa_recv.at[which, r, step])
        return remote(out.at[r, to], into.at[r, source if arriving else me], *sems, (rec, to))

    def aa_start(which, out, into, r, step):
        aa(which, out, into, r, step).start()

    def aa_wait(which, out, into, r):
        for step in range(1, PEERS):
            aa(which, out, into, r, step, True).wait_recv()

    def wo_set(q, c, half=None):
        width = 768 if half is None else 384
        start = c * 768 + (0 if half is None else half * 384)
        return wo.at[
            :,
            pl.ds(pl.multiple_of(lax.rem(q + 4, 4) * 48, 16), 48),
            pl.ds(pl.multiple_of(start, 128), width),
        ]

    def wo_copy(index, arriving=False):
        sems = (wo_send.at[index], wo_recv.at[index])
        if index < 7:
            step = index + 1
            to, source = lax.rem(me + step, PEERS), lax.rem(me + PEERS - step, PEERS)
            mine = wo.at[me, wo_rows, wo_cols]
            landed = wo.at[source, wo_rows, wo_cols]
            device = (rec, to)
        elif index < 13:
            q_sent, half, q_land, to = [
                (quarter, 0, quarter - 1, z_up),
                (quarter, 1, quarter + 1, z_dn),
                (quarter, 1, quarter - 1, z_up),
                (quarter, 0, quarter + 1, z_dn),
                (quarter - 1, 0, quarter - 2, z_up),
                (quarter + 1, 1, quarter + 2, z_dn),
            ][index - 7]
            mine, landed = wo_set(q_sent, core, half), wo_set(q_land, core, half)
            device = (to, me)
        else:
            q, half = [
                (quarter, None), (quarter - 1, 0), (quarter + 1, 1), (quarter - 1, 1),
                (quarter + 1, 0), (quarter - 2, 0), (quarter + 2, 1),
            ][index - 13]
            mine, landed = wo_set(q, core, half), wo_set(q, 1 - core, half)
            device = (sibling, me)
        part = landed if arriving else mine
        return remote(part, part, *sems, device)

    def wo_start(*indices):
        for index in indices:
            wo_copy(index).start()

    def wo_wait(*indices):
        for index in indices:
            wo_copy(index, True).wait_recv()

    def first_norm(r):
        nrm[r, me] = norm_rows(x[r].astype(F32), gain1[...].reshape(1, D))

    def project(unit):
        r, part_rows = unit // 2, pl.ds(unit % 2 * 32, 32)

        @pl.loop(0, 3)
        def _(n):
            cols = pl.ds(pl.multiple_of(n * 256, 256), 256)
            part = dot(nrm[r, :, part_rows, :].reshape(256, D), wq[cols, :], NT)
            qkv[:, part_rows, cols] = part.astype(BF16).reshape(PEERS, 32, 256)

        v = qkv[:, part_rows, pl.ds(512, 256)].astype(F32)
        lane = lax.broadcasted_iota(jnp.int32, v.shape, 2)
        ones = jnp.where(lane == CH, 1.0, 0.0)
        vext[0, :, part_rows, :] = jnp.where(lane < DH, v, ones).astype(BF16)
        vext[1, :, part_rows, :] = jnp.where((lane >= DH) & (lane < CH), v, ones).astype(BF16)

    def attend(r):
        valid = lax.broadcasted_iota(jnp.int32, (128, FRAMES), 1) < lengths[r]

        @pl.loop(1, 5)
        def _(turn):
            block = lax.rem(y + turn, 4)
            mixed = []
            for h in range(2):
                q = qkv[pl.ds(2 * block, 2), :, pl.ds(h * 128, 128)].reshape(128, 128).astype(F32)
                query_u = (q + bias_s[0, pl.ds(h, 1), :]).astype(BF16)
                query_v = (q + bias_s[1, pl.ds(h, 1), :]).astype(BF16)
                keys = qkv[:, :, pl.ds(256 + h * 128, 128)].reshape(FRAMES, 128)
                content = dot(query_u, keys, NT)
                window = pos[h, :, pl.ds(pl.multiple_of(384 - block * 128, 128), 640)]
                relative = dot(query_v, window)
                relative = pltpu.roll(relative, 513, 1, stride=1, stride_axis=0)[:, :FRAMES]
                scores = jnp.where(valid, content + relative, -1e30)
                peak = jnp.max(scores, axis=-1, keepdims=True)
                expd = jnp.exp2((scores - peak) * SCALE2).astype(BF16)
                out = dot(expd, vext[h].reshape(FRAMES, 256))
                mixed.append(out / out[:, CH : CH + 1])
            lane = lax.broadcasted_iota(jnp.int32, mixed[0].shape, 1)
            both = jnp.where(lane < DH, mixed[0], mixed[1])[:, :CH].astype(BF16)
            hs[r, 2 * block] = both[:FD]
            hs[r, 2 * block + 1] = both[FD:]
            for to in (2 * block, 2 * block + 1):
                step = lax.rem(to - me + PEERS, PEERS)

                @pl.when(step != 0)
                def _():
                    aa_start(0, hs, hb, r, step)

        hb[r, me] = hs[r, me]

    def out_project(r):
        heads = jnp.concatenate([hb[r, s] for s in range(PEERS)], axis=-1)
        for n in range(3):
            cols = pl.ds(n * 512, 512)
            part = dot(heads, wo[:, :, cols].reshape(D, 512))
            attended[r, :, cols] = (x[r, :, cols].astype(F32) + part).astype(BF16)
        n2[r, me] = norm_rows(attended[r].astype(F32), gain2[...].reshape(1, D))

    def glu(unit):
        r, start = unit // 2, unit % 2 * 32

        @pl.loop(0, 2)
        def _(c):
            rows = n2[r, :, pl.ds(start, 32), :].reshape(256, D)
            both = dot(rows, wg[pl.ds(pl.multiple_of(c * 256, 256), 256), :], NT)
            gated = (both[:, :128] * sigmoid(both[:, 128:])).reshape(PEERS, 32, 128)
            frame = lax.broadcasted_iota(jnp.int32, gated.shape, 0) * FD
            frame += start + lax.broadcasted_iota(jnp.int32, gated.shape, 1)
            gated = jnp.where(frame < lengths[r], gated, 0.0).astype(BF16).astype(F32)
            for s in range(PEERS):
                gp[c, pl.ds(16 + s * FD + start, 32), :] = gated[s]

    def conv_block(r, block):
        for c in range(2):
            total = jnp.zeros((FD, 128), F32)
            for t in range(TAPS):
                total += gp[c, pl.ds(block * FD + t + 1, FD), :] * taps_s[c, pl.ds(t, 1), :]
            s = total * bn_s[0, pl.ds(c, 1), :] + bn_s[1, pl.ds(c, 1), :]
            out = (s * sigmoid(s)).astype(BF16)
            if c == 0:
                cs[r, block, :, pl.ds(0, 128)] = out
            else:
                cs[r, block, :, pl.ds(128, 64)] = out[:, :64]

    def conv(r):
        @pl.loop(1, PEERS)
        def _(step):
            conv_block(r, lax.rem(me + step, PEERS))
            aa_start(1, cs, cb, r, step)

        conv_block(r, me)
        cb[r, me] = cs[r, me]

    def conv_finish(r):
        conv_out[r] = jnp.concatenate([cb[r, s] for s in range(PEERS)], axis=-1)

    def prepare():
        for start in (96, 224, 352, 480):
            wq[pl.ds(start, 32), :] = jnp.zeros((32, D), BF16)
        wq[pl.ds(704, 64), :] = jnp.zeros((64, D), BF16)
        for start in (320, 448):
            wg[pl.ds(start, 64), :] = jnp.zeros((64, D), BF16)
        for h in range(2):
            pos[h, pl.ds(DH, 32), :] = jnp.zeros((32, 2 * FRAMES), BF16)
        bias_s[...] = jnp.zeros_like(bias_s)
        bias_s[0, pl.ds(0, 2), pl.ds(0, DH)] = bias_u[...]
        bias_s[1, pl.ds(0, 2), pl.ds(0, DH)] = bias_v[...]
        for c in range(2):
            gp[c, pl.ds(0, 16), :] = jnp.zeros((16, 128), F32)
            gp[c, pl.ds(16 + FRAMES, 16), :] = jnp.zeros((16, 128), F32)
        odd = jnp.full((1, 256), xh, jnp.int32) == 1
        window = pl.ds(pl.multiple_of((3 * me) // 2 * 128, 128), 256)

        def mine(ref, count):
            part = ref[:, window] if count > 1 else ref[window].reshape(1, 256)
            moved = pltpu.roll(part, 192, 1)
            return jnp.where(jnp.broadcast_to(odd, (count, 256)), moved, part)

        taps = mine(taps_ref, TAPS)
        scale, shift = mine(scale_ref, 1), mine(shift_ref, 1)
        for c in range(2):
            cols = slice(c * 128, c * 128 + 128)
            taps_s[c, pl.ds(0, TAPS), :] = taps[:, cols]
            bn_s[0, pl.ds(c, 1), :] = scale[:, cols]
            bn_s[1, pl.ds(c, 1), :] = shift[:, cols]

    loads[0].wait()
    loads[2].wait()
    first_norm(0)
    pl.semaphore_wait(barrier, PEERS - 1 + 3)
    ag_first(0, nrm, 0, 1)
    loads[1].wait()
    first_norm(1)
    ag_first(0, nrm, 2, 3)
    loads[3].wait()
    wo_start(*range(7))
    for load in loads[4:]:
        load.wait()
    prepare()
    ag_second(0, nrm, 0, 1)
    ag_third(0, nrm, 0)
    ag_second(0, nrm, 2)
    ag_third(0, nrm, 1)
    ag_second(0, nrm, 3)
    wo_wait(*range(7))
    wo_start(7, 8, 9, 10, 13)
    ag_third(0, nrm, 2)
    ag_finish(0, nrm, 0)
    project(0)
    ag_finish(0, nrm, 1)
    project(1)
    ag_third(0, nrm, 3)
    attend(0)
    ag_finish(0, nrm, 2)
    project(2)
    ag_finish(0, nrm, 3)
    project(3)
    wo_wait(7)
    wo_start(11, 14)
    wo_wait(8)
    wo_start(12, 15)
    attend(1)
    wo_wait(9, 10)
    wo_start(16, 17)
    wo_wait(11, 12)
    wo_start(18, 19)
    aa_wait(0, hs, hb, 0)
    wo_wait(*range(13, 20))
    out_project(0)
    ag_first(1, n2, 0, 1)
    aa_wait(0, hs, hb, 1)
    out_project(1)
    ag_first(1, n2, 2, 3)
    ag_second(1, n2, 0, 1)
    ag_third(1, n2, 0)
    ag_second(1, n2, 2)
    ag_third(1, n2, 1)
    ag_second(1, n2, 3)
    ag_third(1, n2, 2)
    ag_finish(1, n2, 0)
    glu(0)
    ag_finish(1, n2, 1)
    glu(1)
    ag_third(1, n2, 3)
    conv(0)
    ag_finish(1, n2, 2)
    glu(2)
    ag_finish(1, n2, 3)
    glu(3)
    conv(1)
    aa_wait(1, cs, cb, 0)
    conv_finish(0)
    aa_wait(1, cs, cb, 1)
    conv_finish(1)

    for index in range(20):
        wo_copy(index).wait_send()
    for unit in range(4):
        for index in range(9):
            ag(0, nrm, unit, index).wait_send()
            ag(1, n2, unit, index).wait_send()
    for r in range(2):
        for step in range(1, PEERS):
            aa(0, hs, hb, r, step).wait_send()
            aa(1, cs, cb, r, step).wait_send()


def on_device(
    frames_in, lengths, ln1_gain, w_qkv, bias_u, bias_v, pos_keys, w_out, ln2_gain, w_glu,
    depth_kernel, bn_scale, bn_shift,
):
    vmem = pl.BlockSpec(memory_space=pltpu.VMEM)
    gathered = pltpu.VMEM((2, PEERS, FD, D), BF16)
    exchanged = pltpu.VMEM((2, PEERS, FD, CH), BF16)
    dma = pltpu.SemaphoreType.DMA
    return pl.pallas_call(
        kernel,
        out_shape=[pltpu.VMEM(frames_in.shape, BF16)] * 2,
        in_specs=[pl.BlockSpec(memory_space=pl.ANY)] * 13,
        out_specs=[vmem, vmem],
        scratch_shapes=[
            pltpu.VMEM((2, FD, D), BF16),
            gathered,
            gathered,
            pltpu.VMEM((768, D), BF16),
            pltpu.VMEM((512, D), BF16),
            pltpu.VMEM((PEERS, CH, D), BF16),
            pltpu.VMEM((2, 128, 2 * FRAMES), BF16),
            pltpu.VMEM((PEERS, FD, 768), BF16),
            pltpu.VMEM((2, PEERS, FD, 256), BF16),
            exchanged,
            exchanged,
            pltpu.VMEM((2, FRAMES + 32, 128), F32),
            exchanged,
            exchanged,
            pltpu.VMEM((2, 8, 128), F32),
            pltpu.VMEM((2, 32, 128), F32),
            pltpu.VMEM((2, 8, 128), F32),
            pltpu.SMEM((2,), jnp.int32),
            pltpu.VMEM((D,), F32),
            pltpu.VMEM((2, DH), F32),
            pltpu.VMEM((2, DH), F32),
            pltpu.VMEM((D,), F32),
            pltpu.VMEM((TAPS, D), F32),
            pltpu.VMEM((D,), F32),
            pltpu.VMEM((D,), F32),
            dma((22,)),
            dma((2, 4, 9)),
            dma((2, 4, 9)),
            dma((2, 2, PEERS)),
            dma((2, 2, PEERS)),
            dma((20,)),
            dma((20,)),
        ],
        compiler_params=pltpu.CompilerParams(
            collective_id=0, has_side_effects=True, vmem_limit_bytes=60 << 20
        ),
    )(
        frames_in, lengths, ln1_gain, w_qkv, bias_u, bias_v, pos_keys, w_out, ln2_gain, w_glu,
        depth_kernel, bn_scale, bn_shift,
    )


def solution(mesh):
    placed = (
        P("rec", "tm", None),
        P("rec"),
        P(),
        P(None, "tm", None),
        P("tm", None),
        P("tm", None),
        P("tm", None),
        P("tm", None),
        P(),
        P(None, "tm", None),
        P(),
        P(),
        P(),
    )
    return jax.shard_map(
        on_device,
        mesh=mesh,
        in_specs=placed,
        out_specs=(P("rec", "tm", None), P("rec", "tm", None)),
        check_vma=False,
    )
```
